32 devices in a mesh: req: 16 (over z, y, x), head: 2 (over core).
Axes of the slice: x: 2, y: 2, z: 4, core: 2. Of those that a mesh axis runs over, the one named last changes fastest.
Arguments:
- queries: bfloat16 [2, 16, 128, 576], P(None, 'req', 'head'), may hold values from -100 to 100
- prompt_cache: bfloat16 [8192, 576], P('req'), may hold values from -10 to 10
- suffix_cache: bfloat16 [16, 8, 64, 576], P('req'), may hold values from -14 to 14
- new_latent: bfloat16 [2, 16, 576], P(None, 'req'), may hold values from -16 to 16
- suffix_len: int32 [16], P('req'), may hold values from 1 to 512, 4352 in all
- parent: int32 [16], P('req'), may hold values from 0 to 15
- fork_pages: int32 [16, 2], P('req'), may hold values from 0 to 7
Outputs:
- attended: bfloat16 [2, 16, 128, 512], P(None, 'req', 'head')
The draws below stay inside these ranges and needn't reach their ends.
Inputs may be any that keep to these rules, and one draw needn't show every extreme that they name: `suffix_len`: every beam has at least one valid own token.
All inputs are finite; a program needn't handle non-finite values. No bound on the sum of `suffix_len` on one device may be relied on, other than what follows from the above.
Results may differ from the reference program's by a relative error of at most 0.008.
Values may be sent and summed in bfloat16 or wider, within the bound.
A program may use at most 64 MiB of HBM per device.

```python
import math
import jax
import jax.numpy as jnp
import numpy as np
from jax import lax

DL = 512
DR = 64
HEADS = 128
BEAM_DEV = 1
BEAMS = 16
PROMPT_DEV = 512
PROMPT = 8192
PAGE = 64
SUFFIX_PAGES = 8
FORKS = 2
STEPS = 2
N_REQ = 16


def draw_queries(key, part):
    shape = (STEPS, BEAMS, HEADS, DL + DR)
    values = jnp.clip(jax.random.normal(key, shape, jnp.float32), -6.0, 6.0)
    return values.astype(jnp.bfloat16)


def draw_parent(key, part):
    ranks = jax.random.randint(jax.random.fold_in(key, 11), (BEAMS,), 1, BEAMS + 1)
    order = jax.random.permutation(jax.random.fold_in(key, 13), BEAMS).astype(jnp.int32)
    picked = order[BEAMS // ranks - 1]
    beam_index = jnp.arange(BEAMS, dtype=jnp.int32)
    across = (beam_index + BEAMS // 2) % BEAMS
    forced = (beam_index >= BEAMS // 4) & (beam_index <= BEAMS // 2)
    return jnp.where(forced, across, picked).astype(jnp.int32)


def plant(result, stream_key, smallest, largest):
    shape = result.shape
    spot = [jax.random.randint(jax.random.fold_in(stream_key, axis), (), 0, shape[axis]) for axis in range(len(shape))]
    result = result.at[tuple(spot)].set(smallest)
    longest = shape.index(max(shape))
    spot[longest] = (spot[longest] + 1) % shape[longest]
    return result.at[tuple(spot)].set(largest)


def block_levels(stream_key, extent, cuts, least, top_value):
    loudness = 1.0
    for position, shards_of in cuts:
        draws = jax.random.uniform(jax.random.fold_in(jax.random.fold_in(stream_key, 6), position), (shards_of,), jnp.float32, least / len(cuts), top_value / len(cuts))
        loudness = loudness * jnp.repeat(jnp.exp(draws), extent[position] // shards_of).reshape((-1,) + (1,) * (len(extent) - 1 - position))
    return loudness


def profile(count, total, most, slope):
    weights = [(1 << 20) // math.isqrt(rank ** slope) + 1 for rank in range(2, count + 1)]
    surplus, given = total - most - (count - 1), [1] * (count - 1)
    while surplus > 0:
        free = [i for i in range(count - 1) if given[i] < most]
        pool, remaining = sum([weights[i] for i in free]), surplus
        for i in free:
            extra = min(most - given[i], max(1, remaining * weights[i] // pool), surplus)
            given[i] = given[i] + extra
            surplus = surplus - extra
    return np.array([most] + given)


def uneven(rng, count, total, limit, lean):
    if count == 2:
        one = jax.random.randint(rng, (), max(1, total - limit), min(limit, total - 1) + 1)
        return jnp.stack([one, total - one])
    lengths = jnp.asarray(profile(count, total, limit, lean), jnp.int32)
    pairs = (count - 1) // 2
    donor, receiver = lengths[1:1 + 2 * pairs:2], lengths[2:2 + 2 * pairs:2]
    margin = jnp.minimum(donor - 1, limit - receiver)
    passed = jax.random.randint(jax.random.fold_in(rng, 1), (pairs,), 0, 1 << 20) % (margin + 1)
    lengths = lengths.at[1:1 + 2 * pairs:2].set(donor - passed).at[2:2 + 2 * pairs:2].set(receiver + passed)
    return lengths[jax.random.permutation(jax.random.fold_in(rng, 2), count)]


def scatter_about(stream_key, dims, deviation, limit, split=(), held_as=jnp.bfloat16):
    array = deviation * jax.random.normal(stream_key, dims, jnp.float32)
    if split:
        array = array * block_levels(stream_key, dims, split, -0.22, 0.18)
    return jnp.clip(array, -limit, limit).astype(held_as)


def setup_inputs(seed: int = 0) -> dict:
    streams_of = jax.random.split(jax.random.key(seed), 8)
    return {
        "queries": draw_queries(jax.random.fold_in(streams_of[7], 71), 0),
        "prompt_cache": scatter_about(streams_of[1], (PROMPT, DL + DR), 1.6, 10.0, ((0, 16),)),
        "suffix_cache": scatter_about(streams_of[2], (BEAMS, SUFFIX_PAGES, PAGE, DL + DR), 2.2, 14.0, ((0, 16),)),
        "new_latent": scatter_about(streams_of[3], (STEPS, BEAMS, DL + DR), 3.0, 16.0, ((1, 16),)),
        "suffix_len": uneven(streams_of[4], BEAMS, BEAM_DEV * N_REQ * SUFFIX_PAGES * PAGE // 2 + SUFFIX_PAGES * PAGE // 2, SUFFIX_PAGES * PAGE, 2).astype(jnp.int32),
        "parent": draw_parent(jax.random.fold_in(streams_of[7], 71), 0),
        "fork_pages": plant(jax.random.randint(streams_of[6], (BEAMS, FORKS), 0, SUFFIX_PAGES), jax.random.fold_in(streams_of[6], 1), 0, SUFFIX_PAGES - 1).astype(jnp.int32),
    }


score_scale = 192.0 ** -0.5
neg_large = -1.0e30


def prompt_block(rows, keys):
    scores = jnp.dot(rows, keys.T, preferred_element_type=jnp.float32) * score_scale
    top = jnp.max(scores, axis=-1)
    weights = jnp.exp(scores - top[:, None])
    total = jnp.sum(weights, axis=-1)
    summed = jnp.dot(weights.astype(jnp.bfloat16), keys[:, :DL], preferred_element_type=jnp.float32)
    return top, total, (summed / total[:, None]).astype(jnp.bfloat16)


def masked_partial(queries, keys, valid):
    scores = jnp.einsum("sbhk,btk->sbht", queries.astype(jnp.float32), keys.astype(jnp.float32)) * score_scale
    scores = jnp.where(valid, scores, neg_large)
    top = jnp.max(scores, axis=-1)
    weights = jnp.where(valid, jnp.exp(scores - top[..., None]), 0.0)
    total = jnp.sum(weights, axis=-1)
    rounded = lax.optimization_barrier(weights.astype(jnp.bfloat16)).astype(jnp.float32)
    summed = jnp.einsum("sbht,btd->sbhd", rounded, keys[..., :DL].astype(jnp.float32))
    return top, total, summed


def reference(queries, prompt_cache, suffix_cache, new_latent, suffix_len, parent, fork_pages):
    width = DL + DR
    rows = queries.reshape(-1, width)
    count = rows.shape[0]

    def fold(carry, index):
        peak, denom, numer = carry
        keys = lax.dynamic_slice_in_dim(prompt_cache, (index * PROMPT_DEV).astype(jnp.int32), PROMPT_DEV, 0)
        top, total, out = prompt_block(rows, keys)
        wider = lax.optimization_barrier(out).astype(jnp.float32)
        new_peak = jnp.maximum(peak, top)
        factor = jnp.exp(peak - new_peak)
        weight = total * jnp.exp(top - new_peak)
        return (new_peak, denom * factor + weight, numer * factor[:, None] + weight[:, None] * wider), None

    start = (jnp.full((count,), neg_large, jnp.float32), jnp.zeros((count,), jnp.float32), jnp.zeros((count, DL), jnp.float32))
    (peak_p, denom_p, numer_p), _ = lax.scan(fold, start, jnp.arange(N_REQ, dtype=jnp.int32))
    shape = queries.shape[:3]
    peak_p = peak_p.reshape(shape)
    denom_p = denom_p.reshape(shape)
    numer_p = numer_p.reshape(shape + (DL,))

    tiles = suffix_cache[parent[:, None], fork_pages].reshape(BEAMS, FORKS * PAGE, width)
    positions = (fork_pages[:, :, None] * PAGE + jnp.arange(PAGE, dtype=jnp.int32)[None, None, :]).reshape(BEAMS, -1)
    fork_valid = (positions < suffix_len[parent][:, None])[None, :, None, :]
    top_f, total_f, summed_f = masked_partial(queries, tiles, fork_valid)
    out_f = lax.optimization_barrier((summed_f / jnp.maximum(total_f, 1.0)[..., None]).astype(jnp.bfloat16)).astype(jnp.float32)

    own_keys = jnp.concatenate([suffix_cache.reshape(BEAMS, SUFFIX_PAGES * PAGE, width), jnp.swapaxes(new_latent, 0, 1)], axis=1)
    old_valid = jnp.arange(SUFFIX_PAGES * PAGE, dtype=jnp.int32)[None, :] < suffix_len[:, None]
    new_valid = jnp.arange(STEPS, dtype=jnp.int32)[None, :] <= jnp.arange(STEPS, dtype=jnp.int32)[:, None]
    own_valid = jnp.concatenate([jnp.broadcast_to(old_valid[None], (STEPS, BEAMS, SUFFIX_PAGES * PAGE)), jnp.broadcast_to(new_valid[:, None, :], (STEPS, BEAMS, STEPS))], axis=2)[:, :, None, :]
    top_l, total_l, summed_l = masked_partial(queries, own_keys, own_valid)

    peak = jnp.maximum(jnp.maximum(peak_p, top_f), top_l)
    scale_p = jnp.exp(peak_p - peak)
    weight_f = total_f * jnp.exp(top_f - peak)
    weight_l = jnp.exp(top_l - peak)
    denom = denom_p * scale_p + weight_f + total_l * weight_l
    numer = numer_p * scale_p[..., None] + weight_f[..., None] * out_f + weight_l[..., None] * summed_l
    return (numer / denom[..., None]).astype(jnp.bfloat16)
```

```python
import functools

import jax
import jax.numpy as jnp
from jax import lax
from jax.experimental import pallas as pl
from jax.experimental.pallas import tpu as pltpu
from jax.sharding import PartitionSpec as P

DL = 512
PLANE = 4

score_scale = 192.0 ** (-0.5)
neg_large = -1e30
MESH = pl.DeviceIdType.MESH
NT = (((1,), (1,)), ((), ()))


def kernel(
    col_n, head_n, steps_n, forks_n,
    q_hbm, prompt_hbm, suf_hbm, new_ref, len_ref, parent_ref, pages_ref,
    out_ref,
    q_all, prompt_all, suf_all, meta_own, meta_col, meta_plane, col_smem, plane_smem,
    top_ref, total_ref, acc_ref, out_send, stat_send, out_recv, stat_recv,
    local_sem, q_send, q_recv, mc_send, mc_recv, mp_send, mp_recv,
    p_send, p_recv, ps_send, ps_recv, s_send, s_recv, ss_send, ss_recv,
    o_send, o_recv, t_send, t_recv,
):
    req, head = lax.axis_index("req"), lax.axis_index("head")
    col, spot = req // PLANE, req % PLANE
    py, px = spot // 2, spot % 2
    odd = head % 2
    rows = q_hbm.shape[0]
    block = prompt_hbm.shape[0]
    pages_n, page_len, width = suf_hbm.shape
    own_n = pages_n * page_len
    piece, page_piece = block // head_n, pages_n // head_n

    def plane_peer(flip_y, flip_x):
        return col * PLANE + (py + flip_y * (1 - 2 * py)) * 2 + px + flip_x * (1 - 2 * px)

    first = plane_peer(odd, 1 - odd)
    second = plane_peer(1 - odd, odd)
    slot_first, slot_second = 1 + odd, 2 - odd

    def col_peer(shift):
        return ((col + shift + col_n) % col_n) * PLANE + spot

    def sib(shift):
        return (head + shift) % head_n

    def remote(src, dst, send, recv, to_req, to_head):
        return pltpu.make_async_remote_copy(
            src_ref=src, dst_ref=dst, send_sem=send, recv_sem=recv,
            device_id=(to_req, to_head), device_id_type=MESH,
        )

    barrier = pltpu.get_barrier_semaphore()
    for e in range(1, col_n):
        pl.semaphore_signal(barrier, inc=1, device_id=(col_peer(e), head), device_id_type=MESH)
    for d in range(1, PLANE):
        pl.semaphore_signal(
            barrier, inc=1, device_id=(plane_peer(d // 2, d % 2), head), device_id_type=MESH
        )
    for f in range(1, head_n):
        pl.semaphore_signal(barrier, inc=1, device_id=(req, sib(f)), device_id_type=MESH)

    q_here = pltpu.make_async_copy(q_hbm, q_all.at[pl.ds(0, rows)], local_sem.at[0])
    prompt_here = pltpu.make_async_copy(prompt_hbm, prompt_all.at[0], local_sem.at[1])
    suf_here = pltpu.make_async_copy(suf_hbm, suf_all.at[0], local_sem.at[2])
    q_here.start()
    prompt_here.start()
    suf_here.start()

    line = lax.broadcasted_iota(jnp.int32, (8, 128), 0)
    meta = jnp.where(line == 0, parent_ref[0], len_ref[0])
    for k in range(forks_n):
        meta = jnp.where(line == 2 + k, pages_ref[0, k], meta)
    meta_own[...] = meta
    meta_col[0] = meta
    meta_plane[0] = meta

    pl.semaphore_wait(barrier, col_n - 1 + PLANE - 1 + head_n - 1)

    sends = []

    def go(copy):
        copy.start()
        sends.append(copy)
        return copy

    def plane_send(hbm, every, part, send, recv):
        mine = pl.ds(head * part, part)
        return (
            go(remote(hbm.at[mine], every.at[slot_first, mine], send.at[0], recv.at[0], first, head)),
            go(remote(hbm.at[mine], every.at[slot_second, mine], send.at[1], recv.at[1], second, head)),
        )

    def sib_send(every, part, send, recv, kind, slot):
        mine = pl.ds(head * part, part)
        return [
            go(remote(
                every.at[slot, mine], every.at[slot, mine],
                send.at[f - 1, kind], recv.at[f - 1, kind], req, sib(f),
            ))
            for f in range(1, head_n)
        ]

    def pass_on(every, part, send, recv):
        mine = pl.ds(head * part, part)
        return go(remote(
            every.at[slot_first, mine], every.at[3, mine], send.at[2], recv.at[2], second, head
        ))

    p_copies = plane_send(prompt_hbm, prompt_all, piece, p_send, p_recv)
    q_copies = [
        go(remote(
            q_hbm, q_all.at[pl.ds(e * rows, rows)], q_send.at[e - 1], q_recv.at[e - 1],
            col_peer(e), head,
        ))
        for e in range(1, col_n)
    ]
    mc_copies = [
        go(remote(
            meta_own, meta_col.at[e], mc_send.at[e - 1], mc_recv.at[e - 1], col_peer(e), head
        ))
        for e in range(1, col_n)
    ]
    mp_copies = [
        go(remote(
            meta_own, meta_plane.at[d], mp_send.at[d - 1], mp_recv.at[d - 1],
            plane_peer(d // 2, d % 2), head,
        ))
        for d in range(1, PLANE)
    ]

    def attend(start, count, keys, valid=None, initial=False):
        there = pl.ds(start, count)
        scores = (
            lax.dot_general(q_all[there], keys, NT, preferred_element_type=jnp.float32)
            * score_scale
        )
        if valid is not None:
            scores = jnp.where(valid, scores, neg_large)
        top = jnp.max(scores, axis=-1, keepdims=True)
        if not initial:
            old = top_ref[there]
            top = jnp.maximum(top, old)
            factor = jnp.exp(old - top)
        weights = jnp.exp(scores - top)
        if valid is not None:
            weights = jnp.where(valid, weights, 0.0)
        total = jnp.sum(weights, axis=-1, keepdims=True)
        summed = jnp.dot(
            weights.astype(jnp.bfloat16), keys[:, :DL], preferred_element_type=jnp.float32
        )
        if not initial:
            total = total + total_ref[there] * factor
            summed = summed + acc_ref[there] * factor
        top_ref[there] = top
        total_ref[there] = total
        acc_ref[there] = summed

    q_here.wait()
    prompt_here.wait()
    attend(0, rows, prompt_all[0], initial=True)
    suf_here.wait()
    token = lax.broadcasted_iota(jnp.int32, (1, own_n), 1)
    attend(0, rows, suf_all[0].reshape(own_n, width), token < len_ref[0])
    fresh = new_ref[...].astype(jnp.float32)
    line_new = lax.broadcasted_iota(jnp.int32, (128, width), 0)
    new_keys = jnp.zeros((128, width), jnp.float32)
    for t in range(steps_n):
        new_keys = jnp.where(line_new == t, fresh[t : t + 1], new_keys)
    row = lax.broadcasted_iota(jnp.int32, (rows, 128), 0)
    lane = lax.broadcasted_iota(jnp.int32, (rows, 128), 1)
    attend(0, rows, new_keys.astype(jnp.bfloat16), lane <= row // (rows // steps_n))

    p_copies[0].wait_recv()
    p_pass = pass_on(prompt_all, piece, p_send, p_recv)
    sibs = sib_send(prompt_all, piece, ps_send, ps_recv, 0, slot_first)
    p_copies[1].wait_recv()
    sibs += sib_send(prompt_all, piece, ps_send, ps_recv, 1, slot_second)
    s_copies = plane_send(suf_hbm, suf_all, page_piece, s_send, s_recv)
    for copy in sibs:
        copy.wait_recv()
    attend(0, rows, prompt_all[1])
    attend(0, rows, prompt_all[2])
    p_pass.wait_recv()
    last_sibs = sib_send(prompt_all, piece, ps_send, ps_recv, 2, 3)

    others = (col_n - 1) * rows
    for copy in q_copies:
        copy.wait_recv()
    attend(rows, others, prompt_all[0], initial=True)
    for copy in last_sibs:
        copy.wait_recv()
    attend(0, rows, prompt_all[3])

    s_copies[0].wait_recv()
    s_pass = pass_on(suf_all, page_piece, s_send, s_recv)
    sibs = sib_send(suf_all, page_piece, ss_send, ss_recv, 0, slot_first)
    s_copies[1].wait_recv()
    sibs += sib_send(suf_all, page_piece, ss_send, ss_recv, 1, slot_second)
    attend(rows, others, prompt_all[1])
    attend(rows, others, prompt_all[2])
    s_pass.wait_recv()
    sibs += sib_send(suf_all, page_piece, ss_send, ss_recv, 2, 3)
    for copy in mc_copies + mp_copies:
        copy.wait_recv()
    col_down = pltpu.make_async_copy(meta_col, col_smem, local_sem.at[3])
    plane_down = pltpu.make_async_copy(meta_plane, plane_smem, local_sem.at[4])
    col_down.start()
    plane_down.start()
    attend(rows, others, prompt_all[3])
    col_down.wait()
    plane_down.wait()
    for copy in sibs:
        copy.wait_recv()

    diagonal = row == lane

    def as_line(column):
        return jnp.sum(jnp.where(diagonal, column, 0.0), axis=0, keepdims=True)

    def as_column(values):
        return jnp.sum(jnp.where(diagonal, values, 0.0), axis=1, keepdims=True)

    within = lax.broadcasted_iota(jnp.int32, (1, page_len), 1)

    def attend_fork(e):
        beam = col_smem[e, 0, 0]
        beam_col, beam_spot = beam // PLANE, beam % PLANE
        slot = jnp.abs(beam_spot % 2 - px) + 2 * jnp.abs(beam_spot // 2 - py)
        length = jnp.where(beam_col == col, plane_smem[slot, 1, 0], 0)
        keys = []
        for k in range(forks_n):
            page = col_smem[e, 2 + k, 0]
            keys.append(suf_all[slot, page])
        limit = jnp.concatenate(
            [within + col_smem[e, 2 + k, 0] * page_len for k in range(forks_n)], axis=1
        )
        attend(e * rows, rows, jnp.concatenate(keys, axis=0), limit < length)

    stat_line = lax.broadcasted_iota(jnp.int32, (8, 128), 0)
    back = []
    for e in range(1, col_n):
        attend_fork(e)
        there = pl.ds(e * rows, rows)
        top, total = top_ref[there], total_ref[there]
        out_send[e - 1] = (acc_ref[there] / total).astype(jnp.bfloat16)
        stat_send[e - 1] = jnp.where(stat_line == 0, as_line(top), as_line(total))
        back.append((
            go(remote(
                out_send.at[e - 1], out_recv.at[e - 1], o_send.at[e - 1], o_recv.at[e - 1],
                col_peer(-e), head,
            )),
            go(remote(
                stat_send.at[e - 1], stat_recv.at[e - 1], t_send.at[e - 1], t_recv.at[e - 1],
                col_peer(-e), head,
            )),
        ))
    attend_fork(0)

    here = pl.ds(0, rows)
    for e in range(1, col_n):
        for copy in back[e - 1]:
            copy.wait_recv()
        stats = stat_recv[e - 1]
        top_e, total_e = as_column(stats[0:1]), as_column(stats[1:2])
        old = top_ref[here]
        peak = jnp.maximum(old, top_e)
        keep, weight = jnp.exp(old - peak), total_e * jnp.exp(top_e - peak)
        top_ref[here] = peak
        total_ref[here] = total_ref[here] * keep + weight
        acc_ref[here] = acc_ref[here] * keep + out_recv[e - 1].astype(jnp.float32) * weight
    out_ref[...] = (acc_ref[here] / total_ref[here]).astype(jnp.bfloat16)
    for copy in sends:
        copy.wait_send()


def on_device(
    col_n, head_n, queries, prompt_cache, suffix_cache, new_latent, suffix_len, parent, fork_pages
):
    steps_n, beam_dev, head_dev, width = queries.shape
    pages_n, page_len = suffix_cache.shape[1:3]
    block = prompt_cache.shape[0]
    forks_n = fork_pages.shape[1]
    rows = steps_n * head_dev
    every = col_n * rows
    away = col_n - 1
    hbm = pl.BlockSpec(memory_space=pl.ANY)
    vmem = pl.BlockSpec(memory_space=pltpu.VMEM)
    smem = pl.BlockSpec(memory_space=pltpu.SMEM)
    dma = pltpu.SemaphoreType.DMA
    bf16, f32, i32 = jnp.bfloat16, jnp.float32, jnp.int32
    flops = 2 * every * PLANE * block * (width + DL)
    out = pl.pallas_call(
        functools.partial(kernel, col_n, head_n, steps_n, forks_n),
        out_shape=jax.ShapeDtypeStruct((rows, DL), bf16),
        in_specs=[hbm, hbm, hbm, vmem, smem, smem, smem],
        out_specs=vmem,
        scratch_shapes=[
            pltpu.VMEM((every, width), bf16),
            pltpu.VMEM((PLANE, block, width), bf16),
            pltpu.VMEM((PLANE, pages_n, page_len, width), bf16),
            pltpu.VMEM((8, 128), i32),
            pltpu.VMEM((col_n, 8, 128), i32),
            pltpu.VMEM((PLANE, 8, 128), i32),
            pltpu.SMEM((col_n, 8, 128), i32),
            pltpu.SMEM((PLANE, 8, 128), i32),
            pltpu.VMEM((every, 1), f32),
            pltpu.VMEM((every, 1), f32),
            pltpu.VMEM((every, DL), f32),
            pltpu.VMEM((away, rows, DL), bf16),
            pltpu.VMEM((away, 8, 128), f32),
            pltpu.VMEM((away, rows, DL), bf16),
            pltpu.VMEM((away, 8, 128), f32),
            dma((5,)),
            dma((away,)), dma((away,)),
            dma((away,)), dma((away,)),
            dma((PLANE - 1,)), dma((PLANE - 1,)),
            dma((3,)), dma((3,)),
            dma((head_n - 1, 3)), dma((head_n - 1, 3)),
            dma((3,)), dma((3,)),
            dma((head_n - 1, 3)), dma((head_n - 1, 3)),
            dma((away,)), dma((away,)),
            dma((away,)), dma((away,)),
        ],
        compiler_params=pltpu.CompilerParams(
            collective_id=0, has_side_effects=True, vmem_limit_bytes=48 * 1024 * 1024
        ),
        cost_estimate=pl.CostEstimate(
            flops=flops, bytes_accessed=4 * block * width, transcendentals=every * PLANE * block
        ),
    )(
        queries.reshape(rows, width),
        prompt_cache,
        suffix_cache.reshape(pages_n, page_len, width),
        new_latent.reshape(steps_n, width),
        suffix_len,
        parent,
        fork_pages,
    )
    return out.reshape(steps_n, beam_dev, head_dev, DL)


def solution(mesh):
    placed = (
        P(None, "req", "head", None),
        P("req", None),
        P("req", None, None, None),
        P(None, "req", None),
        P("req"),
        P("req"),
        P("req", None),
    )
    return jax.shard_map(
        functools.partial(on_device, mesh.shape["req"] // PLANE, mesh.shape["head"]),
        mesh=mesh,
        in_specs=placed,
        out_specs=P(None, "req", "head", None),
        check_vma=False,
    )
```

```python
import functools
import math

import jax
import jax.numpy as jnp
from jax import lax
from jax.experimental import pallas as pl
from jax.experimental.pallas import tpu as pltpu
from jax.sharding import PartitionSpec as P

DL = 512
PLANE = 4

score_scale = 192.0 ** (-0.5)
neg_large = -1e30
MESH = pl.DeviceIdType.MESH
NT = (((1,), (1,)), ((), ()))
NN = (((1,), (0,)), ((), ()))


def kernel(
    col_n, head_n, steps_n, forks_n,
    q_hbm, prompt_hbm, suf_hbm, new_ref, info_ref,
    out_ref,
    q_all, prompt_all, suf_all, meta_own, meta_col, meta_plane, col_smem, plane_smem,
    top_ref, total_ref, acc_ref, out_send, stat_send, out_recv, stat_recv,
    local_sem, q_send, q_recv, mc_send, mc_recv, mp_send, mp_recv,
    p_send, p_recv, ps_send, ps_recv, s_send, s_recv, ss_send, ss_recv,
    o_send, o_recv, t_send, t_recv,
):
    req, head = lax.axis_index("req"), lax.axis_index("head")
    col, spot = req // PLANE, req % PLANE
    py, px = spot // 2, spot % 2
    odd = head % 2
    rows = q_hbm.shape[0]
    width_n, block = prompt_hbm.shape
    pages_n, page_len, width = suf_hbm.shape
    own_n = pages_n * page_len
    parts = math.gcd(head_n, width_n // 16, pages_n)
    piece, page_piece = width_n // parts, pages_n // parts
    share, team = head % parts, head - head % parts

    def plane_peer(flip_y, flip_x):
        return col * PLANE + (py + flip_y * (1 - 2 * py)) * 2 + px + flip_x * (1 - 2 * px)

    first = plane_peer(odd, 1 - odd)
    second = plane_peer(1 - odd, odd)
    slot_first, slot_second = 1 + odd, 2 - odd

    def col_peer(shift):
        return ((col + shift + col_n) % col_n) * PLANE + spot

    def sib(shift):
        return team + (share + shift) % parts

    def remote(src, dst, send, recv, to_req, to_head):
        return pltpu.make_async_remote_copy(
            src_ref=src, dst_ref=dst, send_sem=send, recv_sem=recv,
            device_id=(to_req, to_head), device_id_type=MESH,
        )

    barrier = pltpu.get_barrier_semaphore()
    for e in range(1, col_n):
        pl.semaphore_signal(barrier, inc=1, device_id=(col_peer(e), head), device_id_type=MESH)
    for d in range(1, PLANE):
        pl.semaphore_signal(
            barrier, inc=1, device_id=(plane_peer(d // 2, d % 2), head), device_id_type=MESH
        )
    for f in range(1, parts):
        pl.semaphore_signal(barrier, inc=1, device_id=(req, sib(f)), device_id_type=MESH)

    q_here = pltpu.make_async_copy(q_hbm, q_all.at[pl.ds(0, rows)], local_sem.at[0])
    prompt_here = pltpu.make_async_copy(prompt_hbm, prompt_all.at[0], local_sem.at[1])
    suf_here = pltpu.make_async_copy(suf_hbm, suf_all.at[0], local_sem.at[2])
    q_here.start()
    prompt_here.start()
    suf_here.start()

    line = lax.broadcasted_iota(jnp.int32, (8, 128), 0)
    info = info_ref[...]
    meta = jnp.zeros((8, 128), jnp.int32)
    for k in range(2 + forks_n):
        meta = jnp.where(line == k, info[:, k : k + 1], meta)
    meta_own[...] = meta
    meta_col[0] = meta
    meta_plane[0] = meta

    pl.semaphore_wait(barrier, col_n - 1 + PLANE - 1 + parts - 1)

    sends = []

    def go(copy):
        copy.start()
        sends.append(copy)
        return copy

    def plane_send(hbm, every, part, send, recv):
        mine = pl.ds(share * part, part)
        return (
            go(remote(hbm.at[mine], every.at[slot_first, mine], send.at[0], recv.at[0], first, head)),
            go(remote(hbm.at[mine], every.at[slot_second, mine], send.at[1], recv.at[1], second, head)),
        )

    def sib_send(every, part, send, recv, kind, slot):
        mine = pl.ds(share * part, part)
        return [
            go(remote(
                every.at[slot, mine], every.at[slot, mine],
                send.at[f - 1, kind], recv.at[f - 1, kind], req, sib(f),
            ))
            for f in range(1, parts)
        ]

    def pass_on(every, part, send, recv):
        mine = pl.ds(share * part, part)
        return go(remote(
            every.at[slot_first, mine], every.at[3, mine], send.at[2], recv.at[2], second, head
        ))

    p_copies = plane_send(prompt_hbm, prompt_all, piece, p_send, p_recv)
    q_copies = [
        go(remote(
            q_hbm, q_all.at[pl.ds(e * rows, rows)], q_send.at[e - 1], q_recv.at[e - 1],
            col_peer(e), head,
        ))
        for e in range(1, col_n)
    ]
    mc_copies = [
        go(remote(
            meta_own, meta_col.at[e], mc_send.at[e - 1], mc_recv.at[e - 1], col_peer(e), head
        ))
        for e in range(1, col_n)
    ]
    mp_copies = [
        go(remote(
            meta_own, meta_plane.at[d], mp_send.at[d - 1], mp_recv.at[d - 1],
            plane_peer(d // 2, d % 2), head,
        ))
        for d in range(1, PLANE)
    ]

    def attend(start, count, keys, valid=None, initial=False, turned=False):
        there = pl.ds(start, count)
        scores = (
            lax.dot_general(
                q_all[there], keys, NN if turned else NT, preferred_element_type=jnp.float32
            )
            * score_scale
        )
        if valid is not None:
            scores = jnp.where(valid, scores, neg_large)
        top = jnp.max(scores, axis=-1, keepdims=True)
        if not initial:
            old = top_ref[there]
            top = jnp.maximum(top, old)
            factor = jnp.exp(old - top)
        weights = jnp.exp(scores - top)
        if valid is not None:
            weights = jnp.where(valid, weights, 0.0)
        total = jnp.sum(weights, axis=-1, keepdims=True)
        summed = lax.dot_general(
            weights.astype(jnp.bfloat16),
            keys[:DL] if turned else keys[:, :DL],
            NT if turned else NN,
            preferred_element_type=jnp.float32,
        )
        if not initial:
            total = total + total_ref[there] * factor
            summed = summed + acc_ref[there] * factor
        top_ref[there] = top
        total_ref[there] = total
        acc_ref[there] = summed

    def attend_prompt(start, count, slot, initial=False):
        attend(start, count, prompt_all[slot], initial=initial, turned=True)

    q_here.wait()
    prompt_here.wait()
    attend_prompt(0, rows, 0, initial=True)
    suf_here.wait()
    token = lax.broadcasted_iota(jnp.int32, (1, own_n), 1)
    attend(0, rows, suf_all[0].reshape(own_n, width), token < info[:, 1:2])
    fresh = new_ref[...].astype(jnp.float32)
    line_new = lax.broadcasted_iota(jnp.int32, (128, width), 0)
    new_keys = jnp.zeros((128, width), jnp.float32)
    for t in range(steps_n):
        new_keys = jnp.where(line_new == t, fresh[t : t + 1], new_keys)
    row = lax.broadcasted_iota(jnp.int32, (rows, 128), 0)
    lane = lax.broadcasted_iota(jnp.int32, (rows, 128), 1)
    attend(0, rows, new_keys.astype(jnp.bfloat16), lane <= row // (rows // steps_n))

    p_copies[0].wait_recv()
    p_pass = pass_on(prompt_all, piece, p_send, p_recv)
    sibs = sib_send(prompt_all, piece, ps_send, ps_recv, 0, slot_first)
    p_copies[1].wait_recv()
    sibs += sib_send(prompt_all, piece, ps_send, ps_recv, 1, slot_second)
    s_copies = plane_send(suf_hbm, suf_all, page_piece, s_send, s_recv)
    for copy in sibs:
        copy.wait_recv()
    attend_prompt(0, rows, 1)
    attend_prompt(0, rows, 2)
    p_pass.wait_recv()
    last_sibs = sib_send(prompt_all, piece, ps_send, ps_recv, 2, 3)

    group_n = math.gcd(col_n - 1, 3)
    members = (col_n - 1) // group_n
    many = members * rows

    def group_start(g):
        return (1 + g * members) * rows

    for copy in q_copies:
        copy.wait_recv()
    attend_prompt(group_start(0), many, 0, initial=True)
    attend_prompt(group_start(0), many, 1)
    for copy in last_sibs:
        copy.wait_recv()
    s_copies[0].wait_recv()
    s_pass = pass_on(suf_all, page_piece, s_send, s_recv)
    sibs = sib_send(suf_all, page_piece, ss_send, ss_recv, 0, slot_first)
    s_copies[1].wait_recv()
    sibs += sib_send(suf_all, page_piece, ss_send, ss_recv, 1, slot_second)
    attend_prompt(group_start(0), many, 2)
    attend_prompt(group_start(0), many, 3)
    for copy in mc_copies + mp_copies:
        copy.wait_recv()
    col_down = pltpu.make_async_copy(meta_col, col_smem, local_sem.at[3])
    plane_down = pltpu.make_async_copy(meta_plane, plane_smem, local_sem.at[4])
    col_down.start()
    plane_down.start()
    if group_n > 1:
        for slot in range(PLANE):
            attend_prompt(group_start(1), many, slot, initial=slot == 0)
    s_pass.wait_recv()
    sibs += sib_send(suf_all, page_piece, ss_send, ss_recv, 2, 3)
    attend_prompt(0, rows, 3)
    col_down.wait()
    plane_down.wait()
    for copy in sibs:
        copy.wait_recv()

    diagonal = row == lane

    def as_line(column):
        return jnp.sum(jnp.where(diagonal, column, 0.0), axis=0, keepdims=True)

    def as_column(values):
        return jnp.sum(jnp.where(diagonal, values, 0.0), axis=1, keepdims=True)

    within = lax.broadcasted_iota(jnp.int32, (1, page_len), 1)

    def attend_fork(e):
        beam = col_smem[e, 0, 0]
        beam_col, beam_spot = beam // PLANE, beam % PLANE
        slot = jnp.abs(beam_spot % 2 - px) + 2 * jnp.abs(beam_spot // 2 - py)
        length = jnp.where(beam_col == col, plane_smem[slot, 1, 0], 0)
        keys = []
        for k in range(forks_n):
            page = col_smem[e, 2 + k, 0]
            keys.append(suf_all[slot, page])
        limit = jnp.concatenate(
            [within + col_smem[e, 2 + k, 0] * page_len for k in range(forks_n)], axis=1
        )
        attend(e * rows, rows, jnp.concatenate(keys, axis=0), limit < length)

    stat_line = lax.broadcasted_iota(jnp.int32, (8, 128), 0)
    back = []
    for e in range(1, col_n):
        if e > 2 * members and (e - 1) % members == 0:
            for slot in range(PLANE):
                attend_prompt(group_start((e - 1) // members), many, slot, initial=slot == 0)
        attend_fork(e)
        there = pl.ds(e * rows, rows)
        top, total = top_ref[there], total_ref[there]
        out_send[e - 1] = (acc_ref[there] / total).astype(jnp.bfloat16)
        stat_send[e - 1] = jnp.where(stat_line == 0, as_line(top), as_line(total))
        back.append((
            go(remote(
                out_send.at[e - 1], out_recv.at[e - 1], o_send.at[e - 1], o_recv.at[e - 1],
                col_peer(-e), head,
            )),
            go(remote(
                stat_send.at[e - 1], stat_recv.at[e - 1], t_send.at[e - 1], t_recv.at[e - 1],
                col_peer(-e), head,
            )),
        ))
    attend_fork(0)

    here = pl.ds(0, rows)
    for e in range(1, col_n):
        for copy in back[e - 1]:
            copy.wait_recv()
        stats = stat_recv[e - 1]
        top_e, total_e = as_column(stats[0:1]), as_column(stats[1:2])
        old = top_ref[here]
        peak = jnp.maximum(old, top_e)
        keep, weight = jnp.exp(old - peak), total_e * jnp.exp(top_e - peak)
        top_ref[here] = peak
        total_ref[here] = total_ref[here] * keep + weight
        acc_ref[here] = acc_ref[here] * keep + out_recv[e - 1].astype(jnp.float32) * weight
    out_ref[...] = (acc_ref[here] / total_ref[here]).astype(jnp.bfloat16)
    for copy in sends:
        copy.wait_send()


def on_device(
    col_n, head_n, queries, prompt_cache, suffix_cache, new_latent, suffix_len, parent, fork_pages
):
    steps_n, beam_dev, head_dev, width = queries.shape
    pages_n, page_len = suffix_cache.shape[1:3]
    block = prompt_cache.shape[0]
    parts = math.gcd(head_n, width // 16, pages_n)
    forks_n = fork_pages.shape[1]
    rows = steps_n * head_dev
    every = col_n * rows
    away = col_n - 1
    hbm = pl.BlockSpec(memory_space=pl.ANY)
    vmem = pl.BlockSpec(memory_space=pltpu.VMEM)
    dma = pltpu.SemaphoreType.DMA
    bf16, f32, i32 = jnp.bfloat16, jnp.float32, jnp.int32
    flops = 2 * every * PLANE * block * (width + DL)
    info = jnp.concatenate([parent[:, None], suffix_len[:, None], fork_pages], axis=1)
    out = pl.pallas_call(
        functools.partial(kernel, col_n, head_n, steps_n, forks_n),
        out_shape=jax.ShapeDtypeStruct((rows, DL), bf16),
        in_specs=[hbm, hbm, hbm, vmem, vmem],
        out_specs=vmem,
        scratch_shapes=[
            pltpu.VMEM((every, width), bf16),
            pltpu.VMEM((PLANE, width, block), bf16),
            pltpu.VMEM((PLANE, pages_n, page_len, width), bf16),
            pltpu.VMEM((8, 128), i32),
            pltpu.VMEM((col_n, 8, 128), i32),
            pltpu.VMEM((PLANE, 8, 128), i32),
            pltpu.SMEM((col_n, 8, 128), i32),
            pltpu.SMEM((PLANE, 8, 128), i32),
            pltpu.VMEM((every, 1), f32),
            pltpu.VMEM((every, 1), f32),
            pltpu.VMEM((every, DL), f32),
            pltpu.VMEM((away, rows, DL), bf16),
            pltpu.VMEM((away, 8, 128), f32),
            pltpu.VMEM((away, rows, DL), bf16),
            pltpu.VMEM((away, 8, 128), f32),
            dma((5,)),
            dma((away,)), dma((away,)),
            dma((away,)), dma((away,)),
            dma((PLANE - 1,)), dma((PLANE - 1,)),
            dma((3,)), dma((3,)),
            dma((max(parts - 1, 1), 3)), dma((max(parts - 1, 1), 3)),
            dma((3,)), dma((3,)),
            dma((max(parts - 1, 1), 3)), dma((max(parts - 1, 1), 3)),
            dma((away,)), dma((away,)),
            dma((away,)), dma((away,)),
        ],
        compiler_params=pltpu.CompilerParams(
            collective_id=0, has_side_effects=True, vmem_limit_bytes=64 * 1024 * 1024
        ),
        cost_estimate=pl.CostEstimate(
            flops=flops, bytes_accessed=4 * block * width, transcendentals=every * PLANE * block
        ),
    )(
        queries.reshape(rows, width),
        prompt_cache.T,
        suffix_cache.reshape(pages_n, page_len, width),
        new_latent.reshape(steps_n, width),
        info,
    )
    return out.reshape(steps_n, beam_dev, head_dev, DL)


def solution(mesh):
    placed = (
        P(None, "req", "head", None),
        P("req", None),
        P("req", None, None, None),
        P(None, "req", None),
        P("req"),
        P("req"),
        P("req", None),
    )
    return jax.shard_map(
        functools.partial(on_device, mesh.shape["req"] // PLANE, mesh.shape["head"]),
        mesh=mesh,
        in_specs=placed,
        out_specs=P(None, "req", "head", None),
        check_vma=False,
    )
```

```python
import functools
import math

import jax
import jax.numpy as jnp
from jax import lax
from jax.experimental import pallas as pl
from jax.experimental.pallas import tpu as pltpu
from jax.sharding import PartitionSpec as P

DL = 512
PLANE = 4

score_scale = 192.0 ** (-0.5)
neg_large = -1e30
MESH = pl.DeviceIdType.MESH
NT = (((1,), (1,)), ((), ()))
NN = (((1,), (0,)), ((), ()))


def kernel(
    col_n, head_n, steps_n, forks_n,
    q_hbm, prompt_hbm, suf_hbm, new_ref, info_ref, pages_ref,
    out_ref,
    q_all, prompt_all, suf_all, meta_own, meta_col, meta_plane, col_smem, plane_smem,
    top_ref, total_ref, acc_ref, out_send, stat_send, out_recv, stat_recv,
    local_sem, q_send, q_recv, mc_send, mc_recv, mp_send, mp_recv,
    p_send, p_recv, ps_send, ps_recv, s_send, s_recv, ss_send, ss_recv,
    o_send, o_recv, t_send, t_recv,
):
    req, head = lax.axis_index("req"), lax.axis_index("head")
    col, spot = req // PLANE, req % PLANE
    py, px = spot // 2, spot % 2
    odd = head % 2
    rows = q_hbm.shape[0]
    width_n, block = prompt_hbm.shape
    pages_n, page_len, width = suf_hbm.shape
    own_n = pages_n * page_len
    parts = math.gcd(head_n, width_n // 16, pages_n)
    piece, page_piece = width_n // parts, pages_n // parts
    share, team = head % parts, head - head % parts

    def plane_peer(flip_y, flip_x):
        return col * PLANE + (py + flip_y * (1 - 2 * py)) * 2 + px + flip_x * (1 - 2 * px)

    first = plane_peer(odd, 1 - odd)
    second = plane_peer(1 - odd, odd)
    slot_first, slot_second = 1 + odd, 2 - odd

    def col_peer(shift):
        return ((col + shift + col_n) % col_n) * PLANE + spot

    def sib(shift):
        return team + (share + shift) % parts

    def remote(src, dst, send, recv, to_req, to_head):
        return pltpu.make_async_remote_copy(
            src_ref=src, dst_ref=dst, send_sem=send, recv_sem=recv,
            device_id=(to_req, to_head), device_id_type=MESH,
        )

    barrier = pltpu.get_barrier_semaphore()
    for e in range(1, col_n):
        pl.semaphore_signal(barrier, inc=1, device_id=(col_peer(e), head), device_id_type=MESH)
    for d in range(1, PLANE):
        pl.semaphore_signal(
            barrier, inc=1, device_id=(plane_peer(d // 2, d % 2), head), device_id_type=MESH
        )
    for f in range(1, parts):
        pl.semaphore_signal(barrier, inc=1, device_id=(req, sib(f)), device_id_type=MESH)

    q_here = pltpu.make_async_copy(q_hbm, q_all.at[pl.ds(0, rows)], local_sem.at[0])
    prompt_here = pltpu.make_async_copy(prompt_hbm, prompt_all.at[0], local_sem.at[1])
    suf_here = pltpu.make_async_copy(suf_hbm, suf_all.at[0], local_sem.at[2])
    q_here.start()
    prompt_here.start()
    suf_here.start()

    line = lax.broadcasted_iota(jnp.int32, (8, 128), 0)
    info = info_ref[...]
    meta = jnp.where(line == 0, info[:, 0:1], info[:, 1:2])
    pages = pages_ref[...]
    for k in range(forks_n):
        meta = jnp.where(line == 2 + k, pages[:, k : k + 1], meta)
    meta_own[...] = meta
    meta_col[0] = meta
    meta_plane[0] = meta

    pl.semaphore_wait(barrier, col_n - 1 + PLANE - 1 + parts - 1)

    sends = []

    def go(copy):
        copy.start()
        sends.append(copy)
        return copy

    def plane_send(hbm, every, part, send, recv):
        mine = pl.ds(share * part, part)
        return (
            go(remote(hbm.at[mine], every.at[slot_first, mine], send.at[0], recv.at[0], first, head)),
            go(remote(hbm.at[mine], every.at[slot_second, mine], send.at[1], recv.at[1], second, head)),
        )

    def sib_send(every, part, send, recv, kind, slot):
        mine = pl.ds(share * part, part)
        return [
            go(remote(
                every.at[slot, mine], every.at[slot, mine],
                send.at[f - 1, kind], recv.at[f - 1, kind], req, sib(f),
            ))
            for f in range(1, parts)
        ]

    def pass_on(every, part, send, recv):
        mine = pl.ds(share * part, part)
        return go(remote(
            every.at[slot_first, mine], every.at[3, mine], send.at[2], recv.at[2], second, head
        ))

    p_copies = plane_send(prompt_hbm, prompt_all, piece, p_send, p_recv)
    q_copies = [
        go(remote(
            q_hbm, q_all.at[pl.ds(e * rows, rows)], q_send.at[e - 1], q_recv.at[e - 1],
            col_peer(e), head,
        ))
        for e in range(1, col_n)
    ]
    mc_copies = [
        go(remote(
            meta_own, meta_col.at[e], mc_send.at[e - 1], mc_recv.at[e - 1], col_peer(e), head
        ))
        for e in range(1, col_n)
    ]
    mp_copies = [
        go(remote(
            meta_own, meta_plane.at[d], mp_send.at[d - 1], mp_recv.at[d - 1],
            plane_peer(d // 2, d % 2), head,
        ))
        for d in range(1, PLANE)
    ]

    s_copies = plane_send(suf_hbm, suf_all, page_piece, s_send, s_recv)

    def attend(start, count, keys, valid=None, initial=False, turned=False):
        there = pl.ds(start, count)
        scores = (
            lax.dot_general(
                q_all[there], keys, NN if turned else NT, preferred_element_type=jnp.float32
            )
            * score_scale
        )
        if valid is not None:
            scores = jnp.where(valid, scores, neg_large)
        top = jnp.max(scores, axis=-1, keepdims=True)
        if not initial:
            old = top_ref[there]
            top = jnp.maximum(top, old)
            factor = jnp.exp(old - top)
        weights = jnp.exp(scores - top)
        if valid is not None:
            weights = jnp.where(valid, weights, 0.0)
        total = jnp.sum(weights, axis=-1, keepdims=True)
        summed = lax.dot_general(
            weights.astype(jnp.bfloat16),
            keys[:DL] if turned else keys[:, :DL],
            NT if turned else NN,
            preferred_element_type=jnp.float32,
        )
        if not initial:
            total = total + total_ref[there] * factor
            summed = summed + acc_ref[there] * factor
        top_ref[there] = top
        total_ref[there] = total
        acc_ref[there] = summed

    def attend_prompt(start, count, slot, initial=False):
        attend(start, count, prompt_all[slot], initial=initial, turned=True)

    q_here.wait()
    prompt_here.wait()
    attend_prompt(0, rows, 0, initial=True)
    suf_here.wait()
    token = lax.broadcasted_iota(jnp.int32, (1, own_n), 1)
    attend(0, rows, suf_all[0].reshape(own_n, width), token < info[:, 1:2])
    fresh = new_ref[...].astype(jnp.float32)
    line_new = lax.broadcasted_iota(jnp.int32, (128, width), 0)
    new_keys = jnp.zeros((128, width), jnp.float32)
    for t in range(steps_n):
        new_keys = jnp.where(line_new == t, fresh[t : t + 1], new_keys)
    row = lax.broadcasted_iota(jnp.int32, (rows, 128), 0)
    lane = lax.broadcasted_iota(jnp.int32, (rows, 128), 1)
    attend(0, rows, new_keys.astype(jnp.bfloat16), lane <= row // (rows // steps_n))

    p_copies[0].wait_recv()
    p_pass = pass_on(prompt_all, piece, p_send, p_recv)
    sibs = sib_send(prompt_all, piece, ps_send, ps_recv, 0, slot_first)
    p_copies[1].wait_recv()
    sibs += sib_send(prompt_all, piece, ps_send, ps_recv, 1, slot_second)
    for copy in sibs:
        copy.wait_recv()
    attend_prompt(0, rows, 1)
    attend_prompt(0, rows, 2)
    s_copies[0].wait_recv()
    s_pass = pass_on(suf_all, page_piece, s_send, s_recv)
    s_sibs = sib_send(suf_all, page_piece, ss_send, ss_recv, 0, slot_first)
    s_copies[1].wait_recv()
    s_sibs += sib_send(suf_all, page_piece, ss_send, ss_recv, 1, slot_second)
    p_pass.wait_recv()
    sibs = sib_send(prompt_all, piece, ps_send, ps_recv, 2, 3)

    others = (col_n - 1) * rows
    for copy in q_copies:
        copy.wait_recv()
    attend_prompt(rows, others, 0, initial=True)
    attend_prompt(rows, others, 1)
    s_pass.wait_recv()
    s_sibs += sib_send(suf_all, page_piece, ss_send, ss_recv, 2, 3)
    for copy in mc_copies + mp_copies:
        copy.wait_recv()
    col_down = pltpu.make_async_copy(meta_col, col_smem, local_sem.at[3])
    plane_down = pltpu.make_async_copy(meta_plane, plane_smem, local_sem.at[4])
    col_down.start()
    plane_down.start()
    attend_prompt(rows, others, 2)
    for copy in sibs:
        copy.wait_recv()
    attend_prompt(rows, others, 3)
    col_down.wait()
    plane_down.wait()
    for copy in s_sibs:
        copy.wait_recv()

    diagonal = row == lane

    def as_line(column):
        return jnp.sum(jnp.where(diagonal, column, 0.0), axis=0, keepdims=True)

    def as_column(values):
        return jnp.sum(jnp.where(diagonal, values, 0.0), axis=1, keepdims=True)

    within = lax.broadcasted_iota(jnp.int32, (1, page_len), 1)

    def attend_fork(e):
        beam = col_smem[e, 0, 0]
        beam_col, beam_spot = beam // PLANE, beam % PLANE
        slot = jnp.abs(beam_spot % 2 - px) + 2 * jnp.abs(beam_spot // 2 - py)
        length = jnp.where(beam_col == col, plane_smem[slot, 1, 0], 0)
        keys = []
        for k in range(forks_n):
            page = col_smem[e, 2 + k, 0]
            keys.append(suf_all[slot, page])
        limit = jnp.concatenate(
            [within + col_smem[e, 2 + k, 0] * page_len for k in range(forks_n)], axis=1
        )
        attend(e * rows, rows, jnp.concatenate(keys, axis=0), limit < length)

    stat_line = lax.broadcasted_iota(jnp.int32, (8, 128), 0)
    back = []
    for e in range(1, col_n):
        attend_fork(e)
        there = pl.ds(e * rows, rows)
        top, total = top_ref[there], total_ref[there]
        out_send[e - 1] = (acc_ref[there] / total).astype(jnp.bfloat16)
        stat_send[e - 1] = jnp.where(stat_line == 0, as_line(top), as_line(total))
        back.append((
            go(remote(
                out_send.at[e - 1], out_recv.at[e - 1], o_send.at[e - 1], o_recv.at[e - 1],
                col_peer(-e), head,
            )),
            go(remote(
                stat_send.at[e - 1], stat_recv.at[e - 1], t_send.at[e - 1], t_recv.at[e - 1],
                col_peer(-e), head,
            )),
        ))
    attend_prompt(0, rows, 3)
    attend_fork(0)

    here = pl.ds(0, rows)
    for e in range(1, col_n):
        for copy in back[e - 1]:
            copy.wait_recv()
        stats = stat_recv[e - 1]
        top_e, total_e = as_column(stats[0:1]), as_column(stats[1:2])
        old = top_ref[here]
        peak = jnp.maximum(old, top_e)
        keep, weight = jnp.exp(old - peak), total_e * jnp.exp(top_e - peak)
        top_ref[here] = peak
        total_ref[here] = total_ref[here] * keep + weight
        acc_ref[here] = acc_ref[here] * keep + out_recv[e - 1].astype(jnp.float32) * weight
    out_ref[...] = (acc_ref[here] / total_ref[here]).astype(jnp.bfloat16)
    for copy in sends:
        copy.wait_send()


def on_device(
    col_n, head_n, queries, prompt_cache, suffix_cache, new_latent, suffix_len, parent, fork_pages
):
    steps_n, beam_dev, head_dev, width = queries.shape
    pages_n, page_len = suffix_cache.shape[1:3]
    block = prompt_cache.shape[0]
    parts = math.gcd(head_n, width // 16, pages_n)
    forks_n = fork_pages.shape[1]
    rows = steps_n * head_dev
    every = col_n * rows
    away = col_n - 1
    hbm = pl.BlockSpec(memory_space=pl.ANY)
    vmem = pl.BlockSpec(memory_space=pltpu.VMEM)
    dma = pltpu.SemaphoreType.DMA
    bf16, f32, i32 = jnp.bfloat16, jnp.float32, jnp.int32
    flops = 2 * every * PLANE * block * (width + DL)
    info = jnp.concatenate([parent[:, None], suffix_len[:, None]], axis=1)
    out = pl.pallas_call(
        functools.partial(kernel, col_n, head_n, steps_n, forks_n),
        out_shape=jax.ShapeDtypeStruct((rows, DL), bf16),
        in_specs=[hbm, hbm, hbm, vmem, vmem, vmem],
        out_specs=vmem,
        scratch_shapes=[
            pltpu.VMEM((every, width), bf16),
            pltpu.VMEM((PLANE, width, block), bf16),
            pltpu.VMEM((PLANE, pages_n, page_len, width), bf16),
            pltpu.VMEM((8, 128), i32),
            pltpu.VMEM((col_n, 8, 128), i32),
            pltpu.VMEM((PLANE, 8, 128), i32),
            pltpu.SMEM((col_n, 8, 128), i32),
            pltpu.SMEM((PLANE, 8, 128), i32),
            pltpu.VMEM((every, 1), f32),
            pltpu.VMEM((every, 1), f32),
            pltpu.VMEM((every, DL), f32),
            pltpu.VMEM((away, rows, DL), bf16),
            pltpu.VMEM((away, 8, 128), f32),
            pltpu.VMEM((away, rows, DL), bf16),
            pltpu.VMEM((away, 8, 128), f32),
            dma((5,)),
            dma((away,)), dma((away,)),
            dma((away,)), dma((away,)),
            dma((PLANE - 1,)), dma((PLANE - 1,)),
            dma((3,)), dma((3,)),
            dma((max(parts - 1, 1), 3)), dma((max(parts - 1, 1), 3)),
            dma((3,)), dma((3,)),
            dma((max(parts - 1, 1), 3)), dma((max(parts - 1, 1), 3)),
            dma((away,)), dma((away,)),
            dma((away,)), dma((away,)),
        ],
        compiler_params=pltpu.CompilerParams(
            collective_id=0, has_side_effects=True, vmem_limit_bytes=48 * 1024 * 1024
        ),
        cost_estimate=pl.CostEstimate(
            flops=flops, bytes_accessed=4 * block * width, transcendentals=every * PLANE * block
        ),
    )(
        queries.reshape(rows, width),
        prompt_cache.T,
        suffix_cache.reshape(pages_n, page_len, width),
        new_latent.reshape(steps_n, width),
        info,
        fork_pages,
    )
    return out.reshape(steps_n, beam_dev, head_dev, DL)


def solution(mesh):
    placed = (
        P(None, "req", "head", None),
        P("req", None),
        P("req", None, None, None),
        P(None, "req", None),
        P("req"),
        P("req"),
        P("req", None),
    )
    return jax.shard_map(
        functools.partial(on_device, mesh.shape["req"] // PLANE, mesh.shape["head"]),
        mesh=mesh,
        in_specs=placed,
        out_specs=P(None, "req", "head", None),
        check_vma=False,
    )
```

```python
import functools
import math

import jax
import jax.numpy as jnp
from jax import lax
from jax.experimental import pallas as pl
from jax.experimental.pallas import tpu as pltpu
from jax.sharding import PartitionSpec as P

DL = 512
PLANE = 4

score_scale = 192.0 ** (-0.5)
neg_large = -1e30
MESH = pl.DeviceIdType.MESH
NT = (((1,), (1,)), ((), ()))
NN = (((1,), (0,)), ((), ()))


def kernel(
    col_n, head_n, steps_n, forks_n,
    q_hbm, prompt_hbm, suf_hbm, new_ref, info_ref, pages_ref,
    out_ref,
    q_all, prompt_all, suf_all, meta_own, meta_col, meta_plane, col_smem, plane_smem,
    top_ref, total_ref, acc_ref, out_send, stat_send, out_recv, stat_recv,
    local_sem, q_send, q_recv, mc_send, mc_recv, mp_send, mp_recv,
    p_send, p_recv, ps_send, ps_recv, s_send, s_recv, ss_send, ss_recv,
    o_send, o_recv, t_send, t_recv,
):
    req, head = lax.axis_index("req"), lax.axis_index("head")
    col, spot = req // PLANE, req % PLANE
    py, px = spot // 2, spot % 2
    odd = head % 2
    rows = q_hbm.shape[0]
    width_n, block = prompt_hbm.shape
    pages_n, page_len, width = suf_hbm.shape
    own_n = pages_n * page_len
    parts = math.gcd(head_n, width_n // 16, pages_n)
    piece, page_piece = width_n // parts, pages_n // parts
    share, team = head % parts, head - head % parts

    def plane_peer(flip_y, flip_x):
        return col * PLANE + (py + flip_y * (1 - 2 * py)) * 2 + px + flip_x * (1 - 2 * px)

    first = plane_peer(odd, 1 - odd)
    second = plane_peer(1 - odd, odd)
    slot_first, slot_second = 1 + odd, 2 - odd

    def col_peer(shift):
        return ((col + shift + col_n) % col_n) * PLANE + spot

    def sib(shift):
        return team + (share + shift) % parts

    def remote(src, dst, send, recv, to_req, to_head):
        return pltpu.make_async_remote_copy(
            src_ref=src, dst_ref=dst, send_sem=send, recv_sem=recv,
            device_id=(to_req, to_head), device_id_type=MESH,
        )

    barrier = pltpu.get_barrier_semaphore()
    for e in range(1, col_n):
        pl.semaphore_signal(barrier, inc=1, device_id=(col_peer(e), head), device_id_type=MESH)
    for d in range(1, PLANE):
        pl.semaphore_signal(
            barrier, inc=1, device_id=(plane_peer(d // 2, d % 2), head), device_id_type=MESH
        )
    for f in range(1, parts):
        pl.semaphore_signal(barrier, inc=1, device_id=(req, sib(f)), device_id_type=MESH)

    q_here = pltpu.make_async_copy(q_hbm, q_all.at[pl.ds(0, rows)], local_sem.at[0])
    prompt_here = pltpu.make_async_copy(prompt_hbm, prompt_all.at[0], local_sem.at[1])
    suf_here = pltpu.make_async_copy(suf_hbm, suf_all.at[0], local_sem.at[2])
    q_here.start()
    prompt_here.start()
    suf_here.start()

    line = lax.broadcasted_iota(jnp.int32, (8, 128), 0)
    info = info_ref[...]
    meta = jnp.where(line == 0, info[:, 0:1], info[:, 1:2])
    pages = pages_ref[...]
    for k in range(forks_n):
        meta = jnp.where(line == 2 + k, pages[:, k : k + 1], meta)
    meta_own[...] = meta
    meta_col[0] = meta
    meta_plane[0] = meta

    pl.semaphore_wait(barrier, col_n - 1 + PLANE - 1 + parts - 1)

    sends = []

    def go(copy):
        copy.start()
        sends.append(copy)
        return copy

    def plane_send(hbm, every, part, send, recv):
        mine = pl.ds(share * part, part)
        return (
            go(remote(hbm.at[mine], every.at[slot_first, mine], send.at[0], recv.at[0], first, head)),
            go(remote(hbm.at[mine], every.at[slot_second, mine], send.at[1], recv.at[1], second, head)),
        )

    def sib_send(every, part, send, recv, kind, slot):
        mine = pl.ds(share * part, part)
        return [
            go(remote(
                every.at[slot, mine], every.at[slot, mine],
                send.at[f - 1, kind], recv.at[f - 1, kind], req, sib(f),
            ))
            for f in range(1, parts)
        ]

    def pass_on(every, part, send, recv):
        mine = pl.ds(share * part, part)
        return go(remote(
            every.at[slot_first, mine], every.at[3, mine], send.at[2], recv.at[2], second, head
        ))

    p_copies = plane_send(prompt_hbm, prompt_all, piece, p_send, p_recv)
    q_copies = [
        go(remote(
            q_hbm, q_all.at[pl.ds(e * rows, rows)], q_send.at[e - 1], q_recv.at[e - 1],
            col_peer(e), head,
        ))
        for e in range(1, col_n)
    ]
    mc_copies = [
        go(remote(
            meta_own, meta_col.at[e], mc_send.at[e - 1], mc_recv.at[e - 1], col_peer(e), head
        ))
        for e in range(1, col_n)
    ]
    mp_copies = [
        go(remote(
            meta_own, meta_plane.at[d], mp_send.at[d - 1], mp_recv.at[d - 1],
            plane_peer(d // 2, d % 2), head,
        ))
        for d in range(1, PLANE)
    ]

    s_copies = plane_send(suf_hbm, suf_all, page_piece, s_send, s_recv)

    def attend(start, count, keys, valid=None, initial=False, turned=False):
        there = pl.ds(start, count)
        scores = (
            lax.dot_general(
                q_all[there], keys, NN if turned else NT, preferred_element_type=jnp.float32
            )
            * score_scale
        )
        if valid is not None:
            scores = jnp.where(valid, scores, neg_large)
        top = jnp.max(scores, axis=-1, keepdims=True)
        if not initial:
            old = top_ref[there]
            top = jnp.maximum(top, old)
            factor = jnp.exp(old - top)
        weights = jnp.exp(scores - top)
        if valid is not None:
            weights = jnp.where(valid, weights, 0.0)
        total = jnp.sum(weights, axis=-1, keepdims=True)
        summed = lax.dot_general(
            weights.astype(jnp.bfloat16),
            keys[:DL] if turned else keys[:, :DL],
            NT if turned else NN,
            preferred_element_type=jnp.float32,
        )
        if not initial:
            total = total + total_ref[there] * factor
            summed = summed + acc_ref[there] * factor
        top_ref[there] = top
        total_ref[there] = total
        acc_ref[there] = summed

    def attend_prompt(start, count, slot, initial=False):
        attend(start, count, prompt_all[slot], initial=initial, turned=True)

    q_here.wait()
    prompt_here.wait()
    attend_prompt(0, rows, 0, initial=True)
    suf_here.wait()
    token = lax.broadcasted_iota(jnp.int32, (1, own_n), 1)
    attend(0, rows, suf_all[0].reshape(own_n, width), token < info[:, 1:2])
    fresh = new_ref[...].astype(jnp.float32)
    line_new = lax.broadcasted_iota(jnp.int32, (128, width), 0)
    new_keys = jnp.zeros((128, width), jnp.float32)
    for t in range(steps_n):
        new_keys = jnp.where(line_new == t, fresh[t : t + 1], new_keys)
    row = lax.broadcasted_iota(jnp.int32, (rows, 128), 0)
    lane = lax.broadcasted_iota(jnp.int32, (rows, 128), 1)
    attend(0, rows, new_keys.astype(jnp.bfloat16), lane <= row // (rows // steps_n))

    p_copies[0].wait_recv()
    p_pass = pass_on(prompt_all, piece, p_send, p_recv)
    sibs = sib_send(prompt_all, piece, ps_send, ps_recv, 0, slot_first)
    p_copies[1].wait_recv()
    sibs += sib_send(prompt_all, piece, ps_send, ps_recv, 1, slot_second)
    s_copies[0].wait_recv()
    s_pass = pass_on(suf_all, page_piece, s_send, s_recv)
    s_sibs = sib_send(suf_all, page_piece, ss_send, ss_recv, 0, slot_first)
    s_copies[1].wait_recv()
    s_sibs += sib_send(suf_all, page_piece, ss_send, ss_recv, 1, slot_second)
    p_pass.wait_recv()
    last_sibs = sib_send(prompt_all, piece, ps_send, ps_recv, 2, 3)

    others = (col_n - 1) * rows
    for copy in q_copies:
        copy.wait_recv()
    attend_prompt(rows, others, 0, initial=True)
    for copy in sibs:
        copy.wait_recv()
    attend_prompt(rows, others, 1)
    s_pass.wait_recv()
    s_sibs += sib_send(suf_all, page_piece, ss_send, ss_recv, 2, 3)
    for copy in mc_copies + mp_copies:
        copy.wait_recv()
    col_down = pltpu.make_async_copy(meta_col, col_smem, local_sem.at[3])
    plane_down = pltpu.make_async_copy(meta_plane, plane_smem, local_sem.at[4])
    col_down.start()
    plane_down.start()
    attend_prompt(rows, others, 2)
    for copy in last_sibs:
        copy.wait_recv()
    attend_prompt(rows, others, 3)
    col_down.wait()
    plane_down.wait()
    for copy in s_sibs:
        copy.wait_recv()

    diagonal = row == lane

    def as_line(column):
        return jnp.sum(jnp.where(diagonal, column, 0.0), axis=0, keepdims=True)

    def as_column(values):
        return jnp.sum(jnp.where(diagonal, values, 0.0), axis=1, keepdims=True)

    within = lax.broadcasted_iota(jnp.int32, (1, page_len), 1)

    def attend_fork(e):
        beam = col_smem[e, 0, 0]
        beam_col, beam_spot = beam // PLANE, beam % PLANE
        slot = jnp.abs(beam_spot % 2 - px) + 2 * jnp.abs(beam_spot // 2 - py)
        length = jnp.where(beam_col == col, plane_smem[slot, 1, 0], 0)
        keys = []
        for k in range(forks_n):
            page = col_smem[e, 2 + k, 0]
            keys.append(suf_all[slot, page])
        limit = jnp.concatenate(
            [within + col_smem[e, 2 + k, 0] * page_len for k in range(forks_n)], axis=1
        )
        attend(e * rows, rows, jnp.concatenate(keys, axis=0), limit < length)

    stat_line = lax.broadcasted_iota(jnp.int32, (8, 128), 0)
    back = []
    for e in range(1, col_n):
        attend_fork(e)
        there = pl.ds(e * rows, rows)
        top, total = top_ref[there], total_ref[there]
        out_send[e - 1] = (acc_ref[there] / total).astype(jnp.bfloat16)
        stat_send[e - 1] = jnp.where(stat_line == 0, as_line(top), as_line(total))
        back.append((
            go(remote(
                out_send.at[e - 1], out_recv.at[e - 1], o_send.at[e - 1], o_recv.at[e - 1],
                col_peer(-e), head,
            )),
            go(remote(
                stat_send.at[e - 1], stat_recv.at[e - 1], t_send.at[e - 1], t_recv.at[e - 1],
                col_peer(-e), head,
            )),
        ))
    for slot in range(1, PLANE):
        attend_prompt(0, rows, slot)
    attend_fork(0)

    here = pl.ds(0, rows)
    for e in range(1, col_n):
        for copy in back[e - 1]:
            copy.wait_recv()
        stats = stat_recv[e - 1]
        top_e, total_e = as_column(stats[0:1]), as_column(stats[1:2])
        old = top_ref[here]
        peak = jnp.maximum(old, top_e)
        keep, weight = jnp.exp(old - peak), total_e * jnp.exp(top_e - peak)
        top_ref[here] = peak
        total_ref[here] = total_ref[here] * keep + weight
        acc_ref[here] = acc_ref[here] * keep + out_recv[e - 1].astype(jnp.float32) * weight
    out_ref[...] = (acc_ref[here] / total_ref[here]).astype(jnp.bfloat16)
    for copy in sends:
        copy.wait_send()


def on_device(
    col_n, head_n, queries, prompt_cache, suffix_cache, new_latent, suffix_len, parent, fork_pages
):
    steps_n, beam_dev, head_dev, width = queries.shape
    pages_n, page_len = suffix_cache.shape[1:3]
    block = prompt_cache.shape[0]
    parts = math.gcd(head_n, width // 16, pages_n)
    forks_n = fork_pages.shape[1]
    rows = steps_n * head_dev
    every = col_n * rows
    away = col_n - 1
    hbm = pl.BlockSpec(memory_space=pltpu.HBM)
    vmem = pl.BlockSpec(memory_space=pltpu.VMEM)
    dma = pltpu.SemaphoreType.DMA
    bf16, f32, i32 = jnp.bfloat16, jnp.float32, jnp.int32
    flops = 2 * every * PLANE * block * (width + DL)
    info = jnp.concatenate([parent[:, None], suffix_len[:, None]], axis=1)
    out = pl.pallas_call(
        functools.partial(kernel, col_n, head_n, steps_n, forks_n),
        out_shape=jax.ShapeDtypeStruct((rows, DL), bf16),
        in_specs=[hbm, hbm, hbm, vmem, vmem, vmem],
        out_specs=vmem,
        scratch_shapes=[
            pltpu.VMEM((every, width), bf16),
            pltpu.VMEM((PLANE, width, block), bf16),
            pltpu.VMEM((PLANE, pages_n, page_len, width), bf16),
            pltpu.VMEM((8, 128), i32),
            pltpu.VMEM((col_n, 8, 128), i32),
            pltpu.VMEM((PLANE, 8, 128), i32),
            pltpu.SMEM((col_n, 8, 128), i32),
            pltpu.SMEM((PLANE, 8, 128), i32),
            pltpu.VMEM((every, 1), f32),
            pltpu.VMEM((every, 1), f32),
            pltpu.VMEM((every, DL), f32),
            pltpu.VMEM((away, rows, DL), bf16),
            pltpu.VMEM((away, 8, 128), f32),
            pltpu.VMEM((away, rows, DL), bf16),
            pltpu.VMEM((away, 8, 128), f32),
            dma((5,)),
            dma((away,)), dma((away,)),
            dma((away,)), dma((away,)),
            dma((PLANE - 1,)), dma((PLANE - 1,)),
            dma((3,)), dma((3,)),
            dma((max(parts - 1, 1), 3)), dma((max(parts - 1, 1), 3)),
            dma((3,)), dma((3,)),
            dma((max(parts - 1, 1), 3)), dma((max(parts - 1, 1), 3)),
            dma((away,)), dma((away,)),
            dma((away,)), dma((away,)),
        ],
        compiler_params=pltpu.CompilerParams(
            collective_id=0, has_side_effects=True, vmem_limit_bytes=48 * 1024 * 1024
        ),
        cost_estimate=pl.CostEstimate(
            flops=flops, bytes_accessed=4 * block * width, transcendentals=every * PLANE * block
        ),
    )(
        queries.reshape(rows, width),
        prompt_cache.T,
        suffix_cache.reshape(pages_n, page_len, width),
        new_latent.reshape(steps_n, width),
        info,
        fork_pages,
    )
    return out.reshape(steps_n, beam_dev, head_dev, DL)


def solution(mesh):
    placed = (
        P(None, "req", "head", None),
        P("req", None),
        P("req", None, None, None),
        P(None, "req", None),
        P("req"),
        P("req"),
        P("req", None),
    )
    return jax.shard_map(
        functools.partial(on_device, mesh.shape["req"] // PLANE, mesh.shape["head"]),
        mesh=mesh,
        in_specs=placed,
        out_specs=P(None, "req", "head", None),
        check_vma=False,
    )
```
